1024 devices in a mesh: row: 256 (over y_lo, x, z, core), col: 4 (over y_hi).
Axes of the slice: x: 8, y: 8 (y_hi: 4, y_lo: 2; y = y_hi * 2 + y_lo), z: 8, core: 2. Of those that a mesh axis runs over, the one named last changes fastest.
Arguments:
- features: bfloat16 [262144, 512], P('row', 'col'), may hold values from -6 to 6
- tile_vals: bfloat16 [2048, 16, 128, 128], P('row'), may hold values from -0.4375 to 0.4375
- tile_cols: int32 [2048, 16], P('row'), may hold values from 0 to 2047, as said below
- tile_count: int32 [2048], P('row'), may hold values from 2 to 16
- weight: bfloat16 [512, 512], P('col'), may hold values from -0.25 to 0.25
- cotangent: bfloat16 [262144, 512], P('row'), may hold values from -6 to 6
Outputs:
- activated: bfloat16 [262144, 512], P('row', 'col')
- grad_weight: float32 [512, 512], P('col')
The draws below stay inside these ranges and needn't reach their ends.
Inputs may be any that keep to these rules, and one draw needn't show every extreme that they name: Block tile_cols[b, t] is held by a device at most 4 indices away from the one holding row block b: tile_cols[b, t] // 8 - b // 8 lies in -4 to 4. Blocks may repeat within a row block; slots at or beyond tile_count[b] hold valid ids and carry no weight.
All inputs are finite; a program needn't handle non-finite values.
Results may differ from the reference program's by a relative error of at most 0.017.
Values may be sent and summed in bfloat16 or wider, within the bound.
No kernel may reach another device: no remote copies, remote signals or barrier semaphores. Data moves between devices by JAX's collectives and lax.ppermute only.
A program may use at most 32 MiB of HBM per device.

```python
import jax
import jax.numpy as jnp
from jax import lax

TILE = 128
F_IN = 512
F_OUT = 512
MAXT = 16
BAND = 4
BPD = 8
NBLK = 2048
NODES = 262144
N_ROW = 256
N_COL = 4


def draw_tile_cols(key, part):
    key = jax.random.fold_in(key, 11)
    first, second = jax.random.split(key)
    owner = jnp.arange(NBLK, dtype=jnp.int32) // BPD
    offset = jax.random.randint(first, (NBLK, MAXT), -BAND, BAND + 1)
    offset = offset.at[:, 0].set(BAND).at[:, 1].set(-BAND)
    source = jnp.clip(owner[:, None] + offset, 0, N_ROW - 1)
    within = jax.random.randint(second, (NBLK, MAXT), 0, BPD)
    within = within.at[:, 0].set(BPD - 1).at[:, 1].set(0)
    return (source * BPD + within).astype(jnp.int32)


def draw_tile_count(key, part):
    key = jax.random.fold_in(key, 23)
    counts = jax.random.randint(key, (NBLK,), 2, MAXT + 1)
    return counts.at[0].set(MAXT).astype(jnp.int32)


def level_of(own_key, extent, cuts, smallest, high):
    loudness = 1.0
    for axis_at, blocks in cuts:
        heights = jax.random.uniform(jax.random.fold_in(jax.random.fold_in(own_key, 6), axis_at), (blocks,), jnp.float32, smallest / len(cuts), high / len(cuts))
        loudness = loudness * jnp.repeat(jnp.exp(heights), extent[axis_at] // blocks).reshape((-1,) + (1,) * (len(extent) - 1 - axis_at))
    return loudness


def gaussian(own_key, extent, scale, reach, shards=(), held_as=jnp.bfloat16):
    gain = level_of(own_key, extent, shards, -0.22, 0.18) if shards else 1.0
    entries = jax.random.normal(own_key, extent, jnp.float32) * scale * gain
    return jnp.minimum(jnp.maximum(entries, -reach), reach).astype(held_as)


def setup_inputs(seed: int = 0) -> dict:
    streams_of = jax.random.split(jax.random.key(seed), 7)
    return {
        "features": gaussian(streams_of[0], (NODES, F_IN), 1.0, 6.0, ((0, 256), (1, 4))),
        "tile_vals": gaussian(streams_of[1], (NBLK, MAXT, TILE, TILE), 0.03, 0.4375, ((0, 256),)),
        "tile_cols": draw_tile_cols(jax.random.fold_in(streams_of[6], 71), 0),
        "tile_count": draw_tile_count(jax.random.fold_in(streams_of[6], 71), 0),
        "weight": gaussian(streams_of[4], (F_IN, F_OUT), F_IN ** -0.5, 0.25, ((0, 4),)),
        "cotangent": gaussian(streams_of[5], (NODES, F_OUT), 1.0, 6.0, ((0, 256),)),
    }


def reference(features, tile_vals, tile_cols, tile_count, weight, cotangent):
    blocks = features.reshape(NBLK, TILE, F_IN)
    slot_ids = jnp.arange(MAXT, dtype=jnp.int32)

    def one_block(args):
        values, columns, count = args
        picked = blocks[columns].astype(jnp.float32)
        keep = (slot_ids < count).astype(jnp.float32)
        picked = picked * keep[:, None, None]
        return jnp.einsum("tij,tjf->if", values.astype(jnp.float32), picked).astype(jnp.bfloat16)

    aggregated = lax.map(one_block, (tile_vals, tile_cols, tile_count)).reshape(NODES, F_IN)
    group = F_IN // N_COL
    pre = jnp.zeros((NODES, F_OUT), jnp.float32)
    for index in range(N_COL):
        term = jnp.dot(aggregated[:, index * group:(index + 1) * group], weight[index * group:(index + 1) * group], preferred_element_type=jnp.float32)
        rounded = lax.optimization_barrier(term.astype(jnp.bfloat16))
        pre = pre + rounded.astype(jnp.float32)
    sigma = jax.nn.sigmoid(pre)
    activated = (pre * sigma).astype(jnp.bfloat16)
    dpre = (cotangent.astype(jnp.float32) * sigma * (1.0 + pre * (1.0 - sigma))).astype(jnp.bfloat16)
    grad_weight = jnp.dot(aggregated.T, dpre, preferred_element_type=jnp.float32)
    return activated, grad_weight
```

```python
import functools

import jax
import jax.numpy as jnp
from jax import lax
from jax.experimental import pallas as pl
from jax.experimental.pallas import tpu as pltpu
from jax.sharding import Mesh, PartitionSpec as P

ROW = ("y_lo", "x", "z", "core")
NEAR = ("z", "core")
FAR = ("y_lo", "x")
F32 = jnp.float32
BF16 = jnp.bfloat16


def shifted(x, by):
    n = lax.axis_size(ROW)
    return lax.ppermute(x, ROW, [(i + by, i) for i in range(n) if 0 <= i + by < n])


def swapped(x):
    return lax.ppermute(x, "core", [(0, 1), (1, 0)])


def halo(features):
    left2, right2 = shifted(features, -4), shifted(features, 4)
    left, right = shifted(features, -2), shifted(features, 2)
    others = swapped(jnp.stack([left, features, right]))
    core = lax.axis_index("core")
    edge = swapped(jnp.where(core == 0, right2, left2))
    return [(left2, 0), (left, 1), (features, 2), (right, 3), (right2, 4), (others, 5), (edge, 8)]


def slots_of(tile_cols, tile_count, blocks_here):
    device = lax.axis_index(ROW)
    source = tile_cols // blocks_here
    chip = source // 2 - device // 2
    same = source % 2 == device % 2
    other = jnp.where(jnp.abs(chip) == 2, 8, chip + 6)
    group = jnp.where(same, chip + 2, other)
    slot = group * blocks_here + tile_cols % blocks_here
    keep = jnp.arange(tile_cols.shape[1], dtype=jnp.int32)[None, :] < tile_count[:, None]
    return jnp.where(keep, slot, 9 * blocks_here)


def tiles_kernel(starts, slots, *refs):
    pieces = refs[: len(starts)]
    vals_hbm, out, window, vals, piece_sems, vals_sems = refs[len(starts) :]
    blocks, count, tile, cols = vals.shape[0], vals.shape[1], vals.shape[2], window.shape[2]
    copies = [
        pltpu.make_async_copy(piece, window.at[pl.ds(start, piece.shape[0])], piece_sems.at[i])
        for i, (piece, start) in enumerate(zip(pieces, starts))
    ]
    for copy in copies:
        copy.start()
    fetches = [
        pltpu.make_async_copy(vals_hbm.at[b], vals.at[b], vals_sems.at[b]) for b in range(blocks)
    ]
    for fetch in fetches:
        fetch.start()
    window[window.shape[0] - 1] = jnp.zeros((tile, cols), window.dtype)
    for copy in copies:
        copy.wait()
    for b in range(blocks):
        fetches[b].wait()
        total = jnp.zeros((tile, cols), F32)
        for t in range(0, count, 2):
            pair = jnp.concatenate([vals[b, t], vals[b, t + 1]], axis=1)
            rows = jnp.concatenate([window[slots[b, t]], window[slots[b, t + 1]]], axis=0)
            total += jnp.dot(pair, rows, preferred_element_type=F32)
        out[pl.ds(b * tile, tile), :] = total.astype(out.dtype)


def tiles(pieces, slots, tile_vals):
    blocks, count, tile, _ = tile_vals.shape
    cols = pieces[0][0].shape[-1]
    arrays = [x.reshape(-1, tile, cols) for x, _ in pieces]
    starts = [group * blocks for _, group in pieces]
    hbm = pl.BlockSpec(memory_space=pl.ANY)
    return pl.pallas_call(
        functools.partial(tiles_kernel, starts),
        out_shape=jax.ShapeDtypeStruct((blocks * tile, cols), BF16),
        in_specs=[pl.BlockSpec(memory_space=pltpu.SMEM)] + [hbm] * (len(arrays) + 1),
        out_specs=pl.BlockSpec(memory_space=pltpu.VMEM),
        scratch_shapes=[
            pltpu.VMEM((9 * blocks + 1, tile, cols), BF16),
            pltpu.VMEM(tile_vals.shape, BF16),
            pltpu.SemaphoreType.DMA((len(arrays),)),
            pltpu.SemaphoreType.DMA((blocks,)),
        ],
        compiler_params=pltpu.CompilerParams(vmem_limit_bytes=16 << 20),
        cost_estimate=pl.CostEstimate(
            flops=2 * blocks * count * tile * tile * cols, bytes_accessed=7 << 20, transcendentals=0
        ),
    )(slots, *arrays, tile_vals)


def dense_kernel(me, agg, weight, cotangent, activated, grad, act, total):
    step = pl.program_id(0)
    mine = me[0]
    width = activated.shape[1]
    joined = jnp.concatenate([agg[k] for k in range(agg.shape[0])], axis=1)
    pre = jnp.dot(joined, weight[...], preferred_element_type=F32)
    sigma = 0.5 * jnp.tanh(0.5 * pre) + 0.5
    act[...] = pre * sigma
    activated[...] = act[:, pl.ds(pl.multiple_of(mine * width, width), width)].astype(BF16)
    dpre = (cotangent[...].astype(F32) * sigma * (1.0 + pre * (1.0 - sigma))).astype(BF16)
    part = lax.dot_general(agg[mine], dpre, (((0,), (0,)), ((), ())), preferred_element_type=F32)

    @pl.when(step == 0)
    def _():
        total[...] = part

    @pl.when(step > 0)
    def _():
        total[...] += part

    @pl.when(step == pl.num_programs(0) - 1)
    def _():
        grad[...] = total[...].astype(BF16)


def dense(agg, weight, cotangent):
    groups, rows, width = agg.shape
    f_out = weight.shape[1]
    block = 256
    me = lax.axis_index("col").astype(jnp.int32)[None]
    return pl.pallas_call(
        dense_kernel,
        out_shape=(
            jax.ShapeDtypeStruct((rows, f_out // groups), BF16),
            jax.ShapeDtypeStruct((width, f_out), BF16),
        ),
        grid=(rows // block,),
        in_specs=[
            pl.BlockSpec(memory_space=pltpu.SMEM),
            pl.BlockSpec((groups, block, width), lambda i: (0, i, 0)),
            pl.BlockSpec((groups * width, f_out), lambda i: (0, 0)),
            pl.BlockSpec((block, f_out), lambda i: (i, 0)),
        ],
        out_specs=(
            pl.BlockSpec((block, f_out // groups), lambda i: (i, 0)),
            pl.BlockSpec((width, f_out), lambda i: (0, 0)),
        ),
        scratch_shapes=[pltpu.VMEM((block, f_out), F32), pltpu.VMEM((width, f_out), F32)],
        compiler_params=pltpu.CompilerParams(vmem_limit_bytes=16 << 20),
    )(me, agg, weight, cotangent)


def spread(x, axes):
    n = lax.axis_size(axes)
    return lax.all_to_all(jnp.broadcast_to(x[None], (n,) + x.shape), axes, 0, 0, tiled=True)


def summed_over_row(part):
    near = lax.axis_size(NEAR)
    rows, cols = part.shape
    pieces = lax.all_to_all(part.reshape(near, rows // near, cols), NEAR, 0, 0, tiled=True)
    piece = jnp.sum(pieces.astype(F32), 0).astype(BF16)
    whole = jnp.sum(spread(piece, FAR).astype(F32), 0).astype(BF16)
    return spread(whole, NEAR).reshape(rows, cols).astype(F32)


def shards(features, tile_vals, tile_cols, tile_count, weight, cotangent):
    whole_weight = lax.all_gather(weight, "col", axis=0, tiled=True)
    slots = slots_of(tile_cols, tile_count, tile_vals.shape[0])
    aggregated = tiles(halo(features), slots, tile_vals)
    activated, part = dense(spread(aggregated, "col"), whole_weight, cotangent)
    return activated, summed_over_row(part)


def solution(mesh):
    split = Mesh(mesh.devices.reshape(2, 8, 8, 2, 4), ROW + ("col",))
    return jax.shard_map(
        shards,
        mesh=split,
        in_specs=(
            P(ROW, "col"),
            P(ROW, None, None, None),
            P(ROW, None),
            P(ROW),
            P("col", None),
            P(ROW, None),
        ),
        out_specs=(P(ROW, "col"), P("col", None)),
        check_vma=False,
    )
```

```python
import functools

import jax
import jax.numpy as jnp
from jax import lax
from jax.experimental import pallas as pl
from jax.experimental.pallas import tpu as pltpu
from jax.sharding import Mesh, PartitionSpec as P

ROW = ("y_lo", "x", "z", "core")
NEAR = ("z", "core")
FAR = ("y_lo", "x")
F32 = jnp.float32
BF16 = jnp.bfloat16


def shifted(x, by):
    n = lax.axis_size(ROW)
    return lax.ppermute(x, ROW, [(i + by, i) for i in range(n) if 0 <= i + by < n])


def swapped(x):
    return lax.ppermute(x, "core", [(0, 1), (1, 0)])


def halo(features, weight):
    whole_weight = spread(weight, "col")
    left2, right2 = shifted(features, -4), shifted(features, 4)
    left, right = shifted(features, -2), shifted(features, 2)
    core = lax.axis_index("core")
    edge = jnp.where(core == 0, right2, left2)
    zero = whole_weight[0, 0, 0] * 0
    others = swapped(jnp.stack([left, features, right, edge]) + zero)
    pieces = [(left2, 0), (left, 1), (features, 2), (right, 3), (right2, 4), (others, 5)]
    return pieces, whole_weight.reshape(-1, weight.shape[1])


def slots_of(tile_cols, tile_count, blocks_here):
    device = lax.axis_index(ROW)
    source = tile_cols // blocks_here
    chip = source // 2 - device // 2
    same = source % 2 == device % 2
    other = jnp.where(jnp.abs(chip) == 2, 8, chip + 6)
    group = jnp.where(same, chip + 2, other)
    slot = group * blocks_here + tile_cols % blocks_here
    keep = jnp.arange(tile_cols.shape[1], dtype=jnp.int32)[None, :] < tile_count[:, None]
    return jnp.where(keep, slot, 9 * blocks_here)


def tiles_kernel(starts, slots, *refs):
    pieces = refs[: len(starts)]
    vals_hbm, out, window, vals, piece_sems, vals_sems = refs[len(starts) :]
    blocks, count, tile, cols = vals.shape[0], vals.shape[1], vals.shape[2], window.shape[2]
    copies = [
        pltpu.make_async_copy(piece, window.at[pl.ds(start, piece.shape[0])], piece_sems.at[i])
        for i, (piece, start) in enumerate(zip(pieces, starts))
    ]
    for copy in copies:
        copy.start()
    fetches = [
        pltpu.make_async_copy(vals_hbm.at[b], vals.at[b], vals_sems.at[b]) for b in range(blocks)
    ]
    for fetch in fetches:
        fetch.start()
    window[window.shape[0] - 1] = jnp.zeros((tile, cols), window.dtype)
    for copy in copies:
        copy.wait()
    for b in range(blocks):
        fetches[b].wait()
        total = jnp.zeros((tile, cols), F32)
        for t in range(0, count, 2):
            pair = jnp.concatenate([vals[b, t], vals[b, t + 1]], axis=1)
            rows = jnp.concatenate([window[slots[b, t]], window[slots[b, t + 1]]], axis=0)
            total += jnp.dot(pair, rows, preferred_element_type=F32)
        done = total.astype(out.dtype)
        for k in range(out.shape[0]):
            out[k, pl.ds(b * tile, tile), :] = done


def tiles(pieces, slots, tile_vals, times):
    blocks, count, tile, _ = tile_vals.shape
    cols = pieces[0][0].shape[-1]
    arrays = [x.reshape(-1, tile, cols) for x, _ in pieces]
    arrays[2] = pltpu.with_memory_space_constraint(arrays[2], pltpu.HBM)
    starts = [group * blocks for _, group in pieces]
    anywhere = pl.BlockSpec(memory_space=pl.ANY)
    hbm = pl.BlockSpec(memory_space=pltpu.HBM)
    return pl.pallas_call(
        functools.partial(tiles_kernel, starts),
        out_shape=jax.ShapeDtypeStruct((times, blocks * tile, cols), BF16),
        in_specs=[pl.BlockSpec(memory_space=pltpu.SMEM)] + [anywhere] * len(arrays) + [hbm],
        out_specs=pl.BlockSpec(memory_space=pltpu.VMEM),
        scratch_shapes=[
            pltpu.VMEM((9 * blocks + 1, tile, cols), BF16),
            pltpu.VMEM(tile_vals.shape, BF16),
            pltpu.SemaphoreType.DMA((len(arrays),)),
            pltpu.SemaphoreType.DMA((blocks,)),
        ],
        compiler_params=pltpu.CompilerParams(vmem_limit_bytes=16 << 20),
        cost_estimate=pl.CostEstimate(
            flops=2 * blocks * count * tile * tile * cols, bytes_accessed=7 << 20, transcendentals=0
        ),
    )(slots, *arrays, pltpu.with_memory_space_constraint(tile_vals, pltpu.HBM))


def dense_kernel(me, agg, weight, cotangent, activated, grad, act, total):
    step = pl.program_id(0)
    mine = me[0]
    width = activated.shape[1]
    joined = jnp.concatenate([agg[k] for k in range(agg.shape[0])], axis=1)
    pre = jnp.dot(joined, weight[...], preferred_element_type=F32)
    sigma = 0.5 * jnp.tanh(0.5 * pre) + 0.5
    act[...] = pre * sigma
    activated[...] = act[:, pl.ds(pl.multiple_of(mine * width, width), width)].astype(BF16)
    dpre = (cotangent[...].astype(F32) * sigma * (1.0 + pre * (1.0 - sigma))).astype(BF16)
    part = lax.dot_general(agg[mine], dpre, (((0,), (0,)), ((), ())), preferred_element_type=F32)

    @pl.when(step == 0)
    def _():
        total[...] = part

    @pl.when(step > 0)
    def _():
        total[...] += part

    @pl.when(step == pl.num_programs(0) - 1)
    def _():
        grad[...] = total[...].astype(BF16)


def dense(agg, weight, cotangent):
    groups, rows, width = agg.shape
    f_out = weight.shape[1]
    block = 256
    me = lax.axis_index("col").astype(jnp.int32)[None]
    return pl.pallas_call(
        dense_kernel,
        out_shape=(
            jax.ShapeDtypeStruct((rows, f_out // groups), BF16),
            jax.ShapeDtypeStruct((width, f_out), BF16),
        ),
        grid=(rows // block,),
        in_specs=[
            pl.BlockSpec(memory_space=pltpu.SMEM),
            pl.BlockSpec((groups, block, width), lambda i: (0, i, 0)),
            pl.BlockSpec((groups * width, f_out), lambda i: (0, 0)),
            pl.BlockSpec((block, f_out), lambda i: (i, 0)),
        ],
        out_specs=(
            pl.BlockSpec((block, f_out // groups), lambda i: (i, 0)),
            pl.BlockSpec((width, f_out), lambda i: (0, 0)),
        ),
        scratch_shapes=[pltpu.VMEM((block, f_out), F32), pltpu.VMEM((width, f_out), F32)],
        compiler_params=pltpu.CompilerParams(vmem_limit_bytes=16 << 20),
    )(me, agg, weight, cotangent)


def spread(x, axes):
    n = lax.axis_size(axes)
    return exchanged(jnp.broadcast_to(x[None], (n,) + x.shape), axes)


def exchanged(x, axes):
    return lax.all_to_all(x, axes, 0, 0, tiled=True)


def summed_over_row(part):
    near = lax.axis_size(NEAR)
    rows, cols = part.shape
    pieces = exchanged(part.reshape(near, rows // near, cols), NEAR)
    piece = jnp.sum(pieces.astype(F32), 0).astype(BF16)
    whole = jnp.sum(spread(piece, FAR).astype(F32), 0).astype(BF16)
    return spread(whole, NEAR).reshape(rows, cols).astype(F32)


def shards(features, tile_vals, tile_cols, tile_count, weight, cotangent):
    groups = lax.axis_size("col")
    slots = slots_of(tile_cols, tile_count, tile_vals.shape[0])
    pieces, whole_weight = halo(features, weight)
    aggregated = tiles(pieces, slots, tile_vals, groups)
    activated, part = dense(exchanged(aggregated, "col"), whole_weight, cotangent)
    return activated, summed_over_row(part)


def solution(mesh):
    split = Mesh(mesh.devices.reshape(2, 8, 8, 2, 4), ROW + ("col",))
    return jax.shard_map(
        shards,
        mesh=split,
        in_specs=(
            P(ROW, "col"),
            P(ROW, None, None, None),
            P(ROW, None),
            P(ROW),
            P("col", None),
            P(ROW, None),
        ),
        out_specs=(P(ROW, "col"), P("col", None)),
        check_vma=False,
    )
```

```python
import functools

import jax
import jax.numpy as jnp
from jax import lax
from jax.experimental import pallas as pl
from jax.experimental.pallas import tpu as pltpu
from jax.sharding import Mesh, PartitionSpec as P

ROW = ("y_lo", "x", "z", "core")
NEAR = ("z", "core")
FAR = ("y_lo", "x")
F32 = jnp.float32
BF16 = jnp.bfloat16


def shifted(x, by):
    n = lax.axis_size(ROW)
    return lax.ppermute(x, ROW, [(i + by, i) for i in range(n) if 0 <= i + by < n])


def swapped(x):
    return lax.ppermute(x, "core", [(0, 1), (1, 0)])


def halo(features):
    left2, right2 = shifted(features, -4), shifted(features, 4)
    left, right = shifted(features, -2), shifted(features, 2)
    core = lax.axis_index("core")
    edge = jnp.where(core == 0, right2, left2)
    others = swapped(jnp.stack([left, features, right, edge]))
    return [(left2, 0), (left, 1), (features, 2), (right, 3), (right2, 4), (others, 5)]


def slots_of(tile_cols, tile_count, blocks_here):
    device = lax.axis_index(ROW)
    source = tile_cols // blocks_here
    chip = source // 2 - device // 2
    same = source % 2 == device % 2
    other = jnp.where(jnp.abs(chip) == 2, 8, chip + 6)
    group = jnp.where(same, chip + 2, other)
    slot = group * blocks_here + tile_cols % blocks_here
    keep = jnp.arange(tile_cols.shape[1], dtype=jnp.int32)[None, :] < tile_count[:, None]
    return jnp.where(keep, slot, 9 * blocks_here)


def tiles_kernel(starts, slots, *refs):
    pieces = refs[: len(starts)]
    vals_hbm, out, window, vals, piece_sems, vals_sems = refs[len(starts) :]
    blocks, count, tile, cols = vals.shape[0], vals.shape[1], vals.shape[2], window.shape[2]
    copies = [
        pltpu.make_async_copy(piece, window.at[pl.ds(start, piece.shape[0])], piece_sems.at[i])
        for i, (piece, start) in enumerate(zip(pieces, starts))
    ]
    for copy in copies:
        copy.start()
    fetches = [
        pltpu.make_async_copy(vals_hbm.at[b], vals.at[b], vals_sems.at[b]) for b in range(blocks)
    ]
    for fetch in fetches:
        fetch.start()
    window[window.shape[0] - 1] = jnp.zeros((tile, cols), window.dtype)
    for copy in copies:
        copy.wait()
    for b in range(blocks):
        fetches[b].wait()
        total = jnp.zeros((tile, cols), F32)
        for t in range(0, count, 2):
            pair = jnp.concatenate([vals[b, t], vals[b, t + 1]], axis=1)
            rows = jnp.concatenate([window[slots[b, t]], window[slots[b, t + 1]]], axis=0)
            total += jnp.dot(pair, rows, preferred_element_type=F32)
        done = total.astype(out.dtype)
        for k in range(out.shape[0]):
            out[k, pl.ds(b * tile, tile), :] = done


def tiles(pieces, slots, tile_vals, times):
    blocks, count, tile, _ = tile_vals.shape
    cols = pieces[0][0].shape[-1]
    arrays = [x.reshape(-1, tile, cols) for x, _ in pieces]
    arrays[2] = pltpu.with_memory_space_constraint(arrays[2], pltpu.HBM)
    starts = [group * blocks for _, group in pieces]
    anywhere = pl.BlockSpec(memory_space=pl.ANY)
    hbm = pl.BlockSpec(memory_space=pltpu.HBM)
    return pl.pallas_call(
        functools.partial(tiles_kernel, starts),
        out_shape=jax.ShapeDtypeStruct((times, blocks * tile, cols), BF16),
        in_specs=[pl.BlockSpec(memory_space=pltpu.SMEM)] + [anywhere] * len(arrays) + [hbm],
        out_specs=pl.BlockSpec(memory_space=pltpu.VMEM),
        scratch_shapes=[
            pltpu.VMEM((9 * blocks + 1, tile, cols), BF16),
            pltpu.VMEM(tile_vals.shape, BF16),
            pltpu.SemaphoreType.DMA((len(arrays),)),
            pltpu.SemaphoreType.DMA((blocks,)),
        ],
        compiler_params=pltpu.CompilerParams(vmem_limit_bytes=16 << 20),
        cost_estimate=pl.CostEstimate(
            flops=2 * blocks * count * tile * tile * cols, bytes_accessed=7 << 20, transcendentals=0
        ),
    )(slots, *arrays, pltpu.with_memory_space_constraint(tile_vals, pltpu.HBM))


def dense_kernel(me, agg, weight, cotangent, activated, grad, act, total):
    step = pl.program_id(0)
    mine = me[0]
    width = activated.shape[1]
    joined = jnp.concatenate([agg[k] for k in range(agg.shape[0])], axis=1)
    pre = jnp.dot(joined, weight[...].reshape(joined.shape[1], -1), preferred_element_type=F32)
    sigma = 0.5 * jnp.tanh(0.5 * pre) + 0.5
    act[...] = pre * sigma
    activated[...] = act[:, pl.ds(pl.multiple_of(mine * width, width), width)].astype(BF16)
    dpre = (cotangent[...].astype(F32) * sigma * (1.0 + pre * (1.0 - sigma))).astype(BF16)
    part = lax.dot_general(agg[mine], dpre, (((0,), (0,)), ((), ())), preferred_element_type=F32)

    @pl.when(step == 0)
    def _():
        total[...] = part

    @pl.when(step > 0)
    def _():
        total[...] += part

    @pl.when(step == pl.num_programs(0) - 1)
    def _():
        grad[...] = total[...].astype(BF16)


def dense(agg, weight, cotangent):
    groups, rows, width = agg.shape
    f_out = weight.shape[-1]
    block = 256
    me = lax.axis_index("col").astype(jnp.int32)[None]
    return pl.pallas_call(
        dense_kernel,
        out_shape=(
            jax.ShapeDtypeStruct((rows, f_out // groups), BF16),
            jax.ShapeDtypeStruct((width, f_out), BF16),
        ),
        grid=(rows // block,),
        in_specs=[
            pl.BlockSpec(memory_space=pltpu.SMEM),
            pl.BlockSpec((groups, block, width), lambda i: (0, i, 0)),
            pl.BlockSpec((groups, width, f_out), lambda i: (0, 0, 0)),
            pl.BlockSpec((block, f_out), lambda i: (i, 0)),
        ],
        out_specs=(
            pl.BlockSpec((block, f_out // groups), lambda i: (i, 0)),
            pl.BlockSpec((width, f_out), lambda i: (0, 0)),
        ),
        scratch_shapes=[pltpu.VMEM((block, f_out), F32), pltpu.VMEM((width, f_out), F32)],
        compiler_params=pltpu.CompilerParams(vmem_limit_bytes=16 << 20),
    )(me, agg, weight, cotangent)


def spread(x, axes):
    n = lax.axis_size(axes)
    return exchanged(jnp.broadcast_to(x[None], (n,) + x.shape), axes)


def exchanged(x, axes):
    return lax.all_to_all(x, axes, 0, 0, tiled=True)


def summed_over_row(part):
    near = lax.axis_size(NEAR)
    rows, cols = part.shape
    pieces = exchanged(part.reshape(near, rows // near, cols), NEAR)
    piece = jnp.sum(pieces.astype(F32), 0).astype(BF16)
    whole = jnp.sum(spread(piece, FAR).astype(F32), 0).astype(BF16)
    return spread(whole, NEAR).reshape(rows, cols).astype(F32)


def shards(features, tile_vals, tile_cols, tile_count, weight, cotangent):
    groups = lax.axis_size("col")
    slots = slots_of(tile_cols, tile_count, tile_vals.shape[0])
    whole_weight = lax.all_gather(weight, ("y_lo", "core", "col"))
    aggregated = tiles(halo(features), slots, tile_vals, groups)
    activated, part = dense(exchanged(aggregated, "col"), whole_weight, cotangent)
    return activated, summed_over_row(part)


def solution(mesh):
    split = Mesh(mesh.devices.reshape(2, 8, 8, 2, 4), ROW + ("col",))
    return jax.shard_map(
        shards,
        mesh=split,
        in_specs=(
            P(ROW, "col"),
            P(ROW, None, None, None),
            P(ROW, None),
            P(ROW),
            P("col", None),
            P(ROW, None),
        ),
        out_specs=(P(ROW, "col"), P("col", None)),
        check_vma=False,
    )
```

```python
import functools

import jax
import jax.numpy as jnp
from jax import lax
from jax.experimental import pallas as pl
from jax.experimental.pallas import tpu as pltpu
from jax.sharding import Mesh, PartitionSpec as P

ROW = ("y_lo", "x", "z", "core")
NEAR = ("z", "core")
FAR = ("y_lo", "x")
F32 = jnp.float32
BF16 = jnp.bfloat16


def swapped(x):
    return lax.ppermute(x, "core", [(0, 1), (1, 0)])


def passed_on(x):
    n = lax.axis_size(ROW)
    up = [(i, i + 2) for i in range(0, n - 2, 2)]
    down = [(i, i - 2) for i in range(3, n, 2)]
    return lax.ppermute(x, ROW, up + down)


def halo(features, weight):
    other = swapped(features)
    one = passed_on(jnp.stack([features, other]))
    two = passed_on(one)
    whole_weight = spread(weight, "col")
    last = swapped(two[1] + whole_weight[0, 0, 0] * 0)
    pieces = [(features, 0), (other, 1), (one, 2), (two, 4), (swapped(one), 6), (last, 8)]
    return pieces, whole_weight.reshape(-1, weight.shape[1])


def slots_of(tile_cols, tile_count, blocks_here):
    device = lax.axis_index(ROW)
    source = tile_cols // blocks_here
    chip = source // 2 - device // 2
    core = device % 2
    same = source % 2 == core
    second = jnp.where(same, 0, 1)
    own_side = (chip < 0) == (core == 0)
    one = jnp.where(own_side, 2 + second, 7 - second)
    two = jnp.where(own_side, 4 + second, 8)
    distance = jnp.abs(chip)
    group = jnp.where(distance == 0, second, jnp.where(distance == 1, one, two))
    slot = group * blocks_here + tile_cols % blocks_here
    keep = jnp.arange(tile_cols.shape[1], dtype=jnp.int32)[None, :] < tile_count[:, None]
    return jnp.where(keep, slot, 9 * blocks_here)


def tiles_kernel(starts, slots, *refs):
    pieces = refs[: len(starts)]
    vals_hbm, out, window, vals, piece_sems, vals_sems = refs[len(starts) :]
    blocks, count, tile, cols = vals.shape[0], vals.shape[1], vals.shape[2], window.shape[2]
    copies = [
        pltpu.make_async_copy(piece, window.at[pl.ds(start, piece.shape[0])], piece_sems.at[i])
        for i, (piece, start) in enumerate(zip(pieces, starts))
    ]
    for copy in copies:
        copy.start()
    fetches = [
        pltpu.make_async_copy(vals_hbm.at[b], vals.at[b], vals_sems.at[b]) for b in range(blocks)
    ]
    for fetch in fetches:
        fetch.start()
    window[window.shape[0] - 1] = jnp.zeros((tile, cols), window.dtype)
    for copy in copies:
        copy.wait()
    for b in range(blocks):
        fetches[b].wait()
        total = jnp.zeros((tile, cols), F32)
        for t in range(0, count, 2):
            pair = jnp.concatenate([vals[b, t], vals[b, t + 1]], axis=1)
            rows = jnp.concatenate([window[slots[b, t]], window[slots[b, t + 1]]], axis=0)
            total += jnp.dot(pair, rows, preferred_element_type=F32)
        done = total.astype(out.dtype)
        for k in range(out.shape[0]):
            out[k, pl.ds(b * tile, tile), :] = done


def tiles(pieces, slots, tile_vals, times):
    blocks, count, tile, _ = tile_vals.shape
    cols = pieces[0][0].shape[-1]
    arrays = [x.reshape(-1, tile, cols) for x, _ in pieces]
    arrays[0] = pltpu.with_memory_space_constraint(arrays[0], pltpu.HBM)
    arrays[2] = pltpu.with_memory_space_constraint(arrays[2], pltpu.HBM)
    starts = [group * blocks for _, group in pieces]
    anywhere = pl.BlockSpec(memory_space=pl.ANY)
    hbm = pl.BlockSpec(memory_space=pltpu.HBM)
    return pl.pallas_call(
        functools.partial(tiles_kernel, starts),
        out_shape=jax.ShapeDtypeStruct((times, blocks * tile, cols), BF16),
        in_specs=[pl.BlockSpec(memory_space=pltpu.SMEM)] + [anywhere] * len(arrays) + [hbm],
        out_specs=pl.BlockSpec(memory_space=pltpu.VMEM),
        scratch_shapes=[
            pltpu.VMEM((9 * blocks + 1, tile, cols), BF16),
            pltpu.VMEM(tile_vals.shape, BF16),
            pltpu.SemaphoreType.DMA((len(arrays),)),
            pltpu.SemaphoreType.DMA((blocks,)),
        ],
        compiler_params=pltpu.CompilerParams(vmem_limit_bytes=16 << 20),
        cost_estimate=pl.CostEstimate(
            flops=2 * blocks * count * tile * tile * cols, bytes_accessed=7 << 20, transcendentals=0
        ),
    )(slots, *arrays, pltpu.with_memory_space_constraint(tile_vals, pltpu.HBM))


def dense_kernel(me, agg, weight, cotangent, activated, grad, act, total):
    step = pl.program_id(0)
    mine = me[0]
    width = activated.shape[1]
    joined = jnp.concatenate([agg[k] for k in range(agg.shape[0])], axis=1)
    pre = jnp.dot(joined, weight[...], preferred_element_type=F32)
    sigma = 0.5 * jnp.tanh(0.5 * pre) + 0.5
    act[...] = pre * sigma
    activated[...] = act[:, pl.ds(pl.multiple_of(mine * width, width), width)].astype(BF16)
    dpre = (cotangent[...].astype(F32) * sigma * (1.0 + pre * (1.0 - sigma))).astype(BF16)
    part = lax.dot_general(agg[mine], dpre, (((0,), (0,)), ((), ())), preferred_element_type=F32)

    @pl.when(step == 0)
    def _():
        total[...] = part

    @pl.when(step > 0)
    def _():
        total[...] += part

    @pl.when(step == pl.num_programs(0) - 1)
    def _():
        grad[...] = total[...].astype(BF16)


def dense(agg, weight, cotangent):
    groups, rows, width = agg.shape
    f_out = weight.shape[1]
    block = 256
    me = lax.axis_index("col").astype(jnp.int32)[None]
    return pl.pallas_call(
        dense_kernel,
        out_shape=(
            jax.ShapeDtypeStruct((rows, f_out // groups), BF16),
            jax.ShapeDtypeStruct((width, f_out), BF16),
        ),
        grid=(rows // block,),
        in_specs=[
            pl.BlockSpec(memory_space=pltpu.SMEM),
            pl.BlockSpec((groups, block, width), lambda i: (0, i, 0)),
            pl.BlockSpec((groups * width, f_out), lambda i: (0, 0)),
            pl.BlockSpec((block, f_out), lambda i: (i, 0)),
        ],
        out_specs=(
            pl.BlockSpec((block, f_out // groups), lambda i: (i, 0)),
            pl.BlockSpec((width, f_out), lambda i: (0, 0)),
        ),
        scratch_shapes=[pltpu.VMEM((block, f_out), F32), pltpu.VMEM((width, f_out), F32)],
        compiler_params=pltpu.CompilerParams(vmem_limit_bytes=16 << 20),
    )(me, agg, weight, cotangent)


def spread(x, axes):
    n = lax.axis_size(axes)
    return exchanged(jnp.broadcast_to(x[None], (n,) + x.shape), axes)


def exchanged(x, axes):
    return lax.all_to_all(x, axes, 0, 0, tiled=True)


def summed_over_row(part):
    near = lax.axis_size(NEAR)
    rows, cols = part.shape
    pieces = exchanged(part.reshape(near, rows // near, cols), NEAR)
    piece = jnp.sum(pieces.astype(F32), 0).astype(BF16)
    whole = jnp.sum(spread(piece, FAR).astype(F32), 0).astype(BF16)
    return spread(whole, NEAR).reshape(rows, cols).astype(F32)


def shards(features, tile_vals, tile_cols, tile_count, weight, cotangent):
    groups = lax.axis_size("col")
    slots = slots_of(tile_cols, tile_count, tile_vals.shape[0])
    pieces, whole_weight = halo(features, weight)
    aggregated = tiles(pieces, slots, tile_vals, groups)
    activated, part = dense(exchanged(aggregated, "col"), whole_weight, cotangent)
    return activated, summed_over_row(part)


def solution(mesh):
    split = Mesh(mesh.devices.reshape(2, 8, 8, 2, 4), ROW + ("col",))
    return jax.shard_map(
        shards,
        mesh=split,
        in_specs=(
            P(ROW, "col"),
            P(ROW, None, None, None),
            P(ROW, None),
            P(ROW),
            P("col", None),
            P(ROW, None),
        ),
        out_specs=(P(ROW, "col"), P("col", None)),
        check_vma=False,
    )
```

```python
import functools

import jax
import jax.numpy as jnp
from jax import lax
from jax.experimental import pallas as pl
from jax.experimental.pallas import tpu as pltpu
from jax.sharding import Mesh, PartitionSpec as P

ROW = ("y_lo", "x", "z", "core")
NEAR = ("z", "core")
FAR = ("y_lo", "x")
F32 = jnp.float32
BF16 = jnp.bfloat16


def swapped(x):
    return lax.ppermute(x, "core", [(0, 1), (1, 0)])


def passed_on(x):
    n = lax.axis_size(ROW)
    up = [(i, i + 2) for i in range(0, n - 2, 2)]
    down = [(i, i - 2) for i in range(3, n, 2)]
    return lax.ppermute(x, ROW, up + down)


def halo(features):
    one = passed_on(features)
    other = swapped(features)
    one_other = passed_on(other)
    two = passed_on(one)
    two_other = passed_on(one_other)
    across = swapped(jnp.stack([one, one_other]))
    last = swapped(two_other)
    arrays = [features, other, one, one_other, two, two_other, across, last]
    return list(zip(arrays, [0, 1, 2, 3, 4, 5, 6, 8]))


def slots_of(tile_cols, tile_count, blocks_here):
    device = lax.axis_index(ROW)
    source = tile_cols // blocks_here
    chip = source // 2 - device // 2
    core = device % 2
    same = source % 2 == core
    second = jnp.where(same, 0, 1)
    own_side = (chip < 0) == (core == 0)
    one = jnp.where(own_side, 2 + second, 7 - second)
    two = jnp.where(own_side, 4 + second, 8)
    distance = jnp.abs(chip)
    group = jnp.where(distance == 0, second, jnp.where(distance == 1, one, two))
    slot = group * blocks_here + tile_cols % blocks_here
    keep = jnp.arange(tile_cols.shape[1], dtype=jnp.int32)[None, :] < tile_count[:, None]
    return jnp.where(keep, slot, 9 * blocks_here)


def tiles_kernel(starts, slots, *refs):
    pieces = refs[: len(starts)]
    vals_hbm, _, out, window, vals, piece_sems, vals_sems = refs[len(starts) :]
    blocks, count, tile, cols = vals.shape[0], vals.shape[1], vals.shape[2], window.shape[2]
    copies = [
        pltpu.make_async_copy(piece, window.at[pl.ds(start, piece.shape[0])], piece_sems.at[i])
        for i, (piece, start) in enumerate(zip(pieces, starts))
    ]
    for copy in copies:
        copy.start()
    fetches = [
        pltpu.make_async_copy(vals_hbm.at[b], vals.at[b], vals_sems.at[b]) for b in range(blocks)
    ]
    for fetch in fetches:
        fetch.start()
    window[window.shape[0] - 1] = jnp.zeros((tile, cols), window.dtype)
    for copy in copies:
        copy.wait()
    for b in range(blocks):
        fetches[b].wait()
        total = jnp.zeros((tile, cols), F32)
        for t in range(0, count, 2):
            pair = jnp.concatenate([vals[b, t], vals[b, t + 1]], axis=1)
            rows = jnp.concatenate([window[slots[b, t]], window[slots[b, t + 1]]], axis=0)
            total += jnp.dot(pair, rows, preferred_element_type=F32)
        done = total.astype(out.dtype)
        for k in range(out.shape[0]):
            out[k, pl.ds(b * tile, tile), :] = done


def tiles(pieces, slots, tile_vals, weight):
    times = weight.shape[0]
    blocks, count, tile, _ = tile_vals.shape
    cols = pieces[0][0].shape[-1]
    arrays = [x.reshape(-1, tile, cols) for x, _ in pieces]
    arrays[0] = pltpu.with_memory_space_constraint(arrays[0], pltpu.HBM)
    arrays[7] = pltpu.with_memory_space_constraint(arrays[7], pltpu.HBM)
    starts = [group * blocks for _, group in pieces]
    anywhere = pl.BlockSpec(memory_space=pl.ANY)
    hbm = pl.BlockSpec(memory_space=pltpu.HBM)
    return pl.pallas_call(
        functools.partial(tiles_kernel, starts),
        out_shape=jax.ShapeDtypeStruct((times, blocks * tile, cols), BF16),
        in_specs=[pl.BlockSpec(memory_space=pltpu.SMEM)] + [anywhere] * len(arrays) + [hbm, anywhere],
        out_specs=pl.BlockSpec(memory_space=pltpu.VMEM),
        scratch_shapes=[
            pltpu.VMEM((9 * blocks + 1, tile, cols), BF16),
            pltpu.VMEM(tile_vals.shape, BF16),
            pltpu.SemaphoreType.DMA((len(arrays),)),
            pltpu.SemaphoreType.DMA((blocks,)),
        ],
        compiler_params=pltpu.CompilerParams(vmem_limit_bytes=16 << 20),
        cost_estimate=pl.CostEstimate(
            flops=2 * blocks * count * tile * tile * cols, bytes_accessed=7 << 20, transcendentals=0
        ),
    )(slots, *arrays, pltpu.with_memory_space_constraint(tile_vals, pltpu.HBM), weight)


def dense_kernel(me, agg, weight, cotangent, activated, grad, act, total):
    step = pl.program_id(0)
    mine = me[0]
    width = activated.shape[1]
    joined = jnp.concatenate([agg[k] for k in range(agg.shape[0])], axis=1)
    pre = jnp.dot(joined, weight[...], preferred_element_type=F32)
    sigma = 0.5 * jnp.tanh(0.5 * pre) + 0.5
    act[...] = pre * sigma
    activated[...] = act[:, pl.ds(pl.multiple_of(mine * width, width), width)].astype(BF16)
    dpre = (cotangent[...].astype(F32) * sigma * (1.0 + pre * (1.0 - sigma))).astype(BF16)
    part = lax.dot_general(agg[mine], dpre, (((0,), (0,)), ((), ())), preferred_element_type=F32)

    @pl.when(step == 0)
    def _():
        total[...] = part

    @pl.when(step > 0)
    def _():
        total[...] += part

    @pl.when(step == pl.num_programs(0) - 1)
    def _():
        grad[...] = total[...].astype(BF16)


def dense(agg, weight, cotangent):
    groups, rows, width = agg.shape
    f_out = weight.shape[1]
    block = 256
    me = lax.axis_index("col").astype(jnp.int32)[None]
    return pl.pallas_call(
        dense_kernel,
        out_shape=(
            jax.ShapeDtypeStruct((rows, f_out // groups), BF16),
            jax.ShapeDtypeStruct((width, f_out), BF16),
        ),
        grid=(rows // block,),
        in_specs=[
            pl.BlockSpec(memory_space=pltpu.SMEM),
            pl.BlockSpec((groups, block, width), lambda i: (0, i, 0)),
            pl.BlockSpec((groups * width, f_out), lambda i: (0, 0)),
            pl.BlockSpec((block, f_out), lambda i: (i, 0)),
        ],
        out_specs=(
            pl.BlockSpec((block, f_out // groups), lambda i: (i, 0)),
            pl.BlockSpec((width, f_out), lambda i: (0, 0)),
        ),
        scratch_shapes=[pltpu.VMEM((block, f_out), F32), pltpu.VMEM((width, f_out), F32)],
        compiler_params=pltpu.CompilerParams(vmem_limit_bytes=16 << 20),
    )(me, agg, weight, cotangent)


def spread(x, axes):
    n = lax.axis_size(axes)
    return exchanged(jnp.broadcast_to(x[None], (n,) + x.shape), axes)


def exchanged(x, axes):
    return lax.all_to_all(x, axes, 0, 0, tiled=True)


def summed_over_row(part):
    near = lax.axis_size(NEAR)
    rows, cols = part.shape
    pieces = exchanged(part.reshape(near, rows // near, cols), NEAR)
    piece = jnp.sum(pieces.astype(F32), 0).astype(BF16)
    whole = jnp.sum(spread(piece, FAR).astype(F32), 0).astype(BF16)
    return spread(whole, NEAR).reshape(rows, cols).astype(F32)


def shards(features, tile_vals, tile_cols, tile_count, weight, cotangent):
    slots = slots_of(tile_cols, tile_count, tile_vals.shape[0])
    whole_weight = spread(weight, "col")
    aggregated = tiles(halo(features), slots, tile_vals, whole_weight)
    whole_weight = whole_weight.reshape(-1, weight.shape[1])
    activated, part = dense(exchanged(aggregated, "col"), whole_weight, cotangent)
    return activated, summed_over_row(part)


def solution(mesh):
    split = Mesh(mesh.devices.reshape(2, 8, 8, 2, 4), ROW + ("col",))
    return jax.shard_map(
        shards,
        mesh=split,
        in_specs=(
            P(ROW, "col"),
            P(ROW, None, None, None),
            P(ROW, None),
            P(ROW),
            P("col", None),
            P(ROW, None),
        ),
        out_specs=(P(ROW, "col"), P("col", None)),
        check_vma=False,
    )
```

```python
import functools

import jax
import jax.numpy as jnp
from jax import lax
from jax.experimental import pallas as pl
from jax.experimental.pallas import tpu as pltpu
from jax.sharding import Mesh, PartitionSpec as P

ROW = ("y_lo", "x", "z", "core")
NEAR = ("z", "core")
FAR = ("y_lo", "x")
F32 = jnp.float32
BF16 = jnp.bfloat16


def swapped(x):
    return lax.ppermute(x, "core", [(0, 1), (1, 0)])


def passed_on(x):
    n = lax.axis_size(ROW)
    up = [(i, i + 2) for i in range(0, n - 2, 2)]
    down = [(i, i - 2) for i in range(3, n, 2)]
    return lax.ppermute(x, ROW, up + down)


def halo(features):
    other = swapped(features)
    one = passed_on(jnp.stack([features, other]))
    two = passed_on(one)
    return [(features, 0), (other, 1), (one, 2), (two, 4), (swapped(one), 6), (swapped(two[1]), 8)]


def slots_of(tile_cols, tile_count, blocks_here):
    device = lax.axis_index(ROW)
    source = tile_cols // blocks_here
    chip = source // 2 - device // 2
    core = device % 2
    same = source % 2 == core
    second = jnp.where(same, 0, 1)
    own_side = (chip < 0) == (core == 0)
    one = jnp.where(own_side, 2 + second, 7 - second)
    two = jnp.where(own_side, 4 + second, 8)
    distance = jnp.abs(chip)
    group = jnp.where(distance == 0, second, jnp.where(distance == 1, one, two))
    slot = group * blocks_here + tile_cols % blocks_here
    keep = jnp.arange(tile_cols.shape[1], dtype=jnp.int32)[None, :] < tile_count[:, None]
    return jnp.where(keep, slot, 9 * blocks_here)


def tiles_kernel(starts, slots, *refs):
    pieces = refs[: len(starts)]
    vals_hbm, out, window, vals, piece_sems, vals_sems = refs[len(starts) :]
    blocks, count, tile, cols = vals.shape[0], vals.shape[1], vals.shape[2], window.shape[2]
    copies = [
        pltpu.make_async_copy(piece, window.at[pl.ds(start, piece.shape[0])], piece_sems.at[i])
        for i, (piece, start) in enumerate(zip(pieces, starts))
    ]
    for copy in copies:
        copy.start()
    fetches = [
        pltpu.make_async_copy(vals_hbm.at[b], vals.at[b], vals_sems.at[b]) for b in range(blocks)
    ]
    for fetch in fetches:
        fetch.start()
    window[window.shape[0] - 1] = jnp.zeros((tile, cols), window.dtype)
    for copy in copies:
        copy.wait()
    for b in range(blocks):
        fetches[b].wait()
        total = jnp.zeros((tile, cols), F32)
        for t in range(0, count, 2):
            pair = jnp.concatenate([vals[b, t], vals[b, t + 1]], axis=1)
            rows = jnp.concatenate([window[slots[b, t]], window[slots[b, t + 1]]], axis=0)
            total += jnp.dot(pair, rows, preferred_element_type=F32)
        done = total.astype(out.dtype)
        for k in range(out.shape[0]):
            out[k, pl.ds(b * tile, tile), :] = done


def tiles(pieces, slots, tile_vals, times):
    blocks, count, tile, _ = tile_vals.shape
    cols = pieces[0][0].shape[-1]
    arrays = [x.reshape(-1, tile, cols) for x, _ in pieces]
    arrays[0] = pltpu.with_memory_space_constraint(arrays[0], pltpu.HBM)
    arrays[2] = pltpu.with_memory_space_constraint(arrays[2], pltpu.HBM)
    starts = [group * blocks for _, group in pieces]
    anywhere = pl.BlockSpec(memory_space=pl.ANY)
    hbm = pl.BlockSpec(memory_space=pltpu.HBM)
    return pl.pallas_call(
        functools.partial(tiles_kernel, starts),
        out_shape=jax.ShapeDtypeStruct((times, blocks * tile, cols), BF16),
        in_specs=[pl.BlockSpec(memory_space=pltpu.SMEM)] + [anywhere] * len(arrays) + [hbm],
        out_specs=pl.BlockSpec(memory_space=pltpu.VMEM),
        scratch_shapes=[
            pltpu.VMEM((9 * blocks + 1, tile, cols), BF16),
            pltpu.VMEM(tile_vals.shape, BF16),
            pltpu.SemaphoreType.DMA((len(arrays),)),
            pltpu.SemaphoreType.DMA((blocks,)),
        ],
        compiler_params=pltpu.CompilerParams(vmem_limit_bytes=16 << 20),
        cost_estimate=pl.CostEstimate(
            flops=2 * blocks * count * tile * tile * cols, bytes_accessed=7 << 20, transcendentals=0
        ),
    )(slots, *arrays, pltpu.with_memory_space_constraint(tile_vals, pltpu.HBM))


def dense_kernel(me, agg, weight, cotangent, activated, grad, act, total):
    step = pl.program_id(0)
    mine = me[0]
    width = activated.shape[1]
    joined = jnp.concatenate([agg[k] for k in range(agg.shape[0])], axis=1)
    pre = jnp.dot(joined, weight[...], preferred_element_type=F32)
    sigma = 0.5 * jnp.tanh(0.5 * pre) + 0.5
    act[...] = pre * sigma
    activated[...] = act[:, pl.ds(pl.multiple_of(mine * width, width), width)].astype(BF16)
    dpre = (cotangent[...].astype(F32) * sigma * (1.0 + pre * (1.0 - sigma))).astype(BF16)
    part = lax.dot_general(agg[mine], dpre, (((0,), (0,)), ((), ())), preferred_element_type=F32)

    @pl.when(step == 0)
    def _():
        total[...] = part

    @pl.when(step > 0)
    def _():
        total[...] += part

    @pl.when(step == pl.num_programs(0) - 1)
    def _():
        grad[...] = total[...].astype(BF16)


def dense(agg, weight, cotangent):
    groups, rows, width = agg.shape
    f_out = weight.shape[1]
    block = 256
    me = lax.axis_index("col").astype(jnp.int32)[None]
    return pl.pallas_call(
        dense_kernel,
        out_shape=(
            jax.ShapeDtypeStruct((rows, f_out // groups), BF16),
            jax.ShapeDtypeStruct((width, f_out), BF16),
        ),
        grid=(rows // block,),
        in_specs=[
            pl.BlockSpec(memory_space=pltpu.SMEM),
            pl.BlockSpec((groups, block, width), lambda i: (0, i, 0)),
            pl.BlockSpec((groups * width, f_out), lambda i: (0, 0)),
            pl.BlockSpec((block, f_out), lambda i: (i, 0)),
        ],
        out_specs=(
            pl.BlockSpec((block, f_out // groups), lambda i: (i, 0)),
            pl.BlockSpec((width, f_out), lambda i: (0, 0)),
        ),
        scratch_shapes=[pltpu.VMEM((block, f_out), F32), pltpu.VMEM((width, f_out), F32)],
        compiler_params=pltpu.CompilerParams(vmem_limit_bytes=16 << 20),
    )(me, agg, weight, cotangent)


def spread(x, axes):
    n = lax.axis_size(axes)
    return exchanged(jnp.broadcast_to(x[None], (n,) + x.shape), axes)


def exchanged(x, axes):
    return lax.all_to_all(x, axes, 0, 0, tiled=True)


def summed_over_row(part):
    near = lax.axis_size(NEAR)
    rows, cols = part.shape
    pieces = exchanged(part.reshape(near, rows // near, cols), NEAR)
    piece = jnp.sum(pieces.astype(F32), 0).astype(BF16)
    whole = jnp.sum(spread(piece, FAR).astype(F32), 0).astype(BF16)
    return spread(whole, NEAR).reshape(rows, cols).astype(F32)


def shards(features, tile_vals, tile_cols, tile_count, weight, cotangent):
    groups = lax.axis_size("col")
    slots = slots_of(tile_cols, tile_count, tile_vals.shape[0])
    whole_weight = spread(weight, "col").reshape(-1, weight.shape[1])
    aggregated = tiles(halo(features), slots, tile_vals, groups)
    activated, part = dense(exchanged(aggregated, "col"), whole_weight, cotangent)
    return activated, summed_over_row(part)


def solution(mesh):
    split = Mesh(mesh.devices.reshape(2, 8, 8, 2, 4), ROW + ("col",))
    return jax.shard_map(
        shards,
        mesh=split,
        in_specs=(
            P(ROW, "col"),
            P(ROW, None, None, None),
            P(ROW, None),
            P(ROW),
            P("col", None),
            P(ROW, None),
        ),
        out_specs=(P(ROW, "col"), P("col", None)),
        check_vma=False,
    )
```

```python
import functools

import jax
import jax.numpy as jnp
from jax import lax
from jax.experimental import pallas as pl
from jax.experimental.pallas import tpu as pltpu
from jax.sharding import Mesh, PartitionSpec as P

ROW = ("y_lo", "x", "z", "core")
NEAR = ("z", "core")
FAR = ("y_lo", "x")
F32 = jnp.float32
BF16 = jnp.bfloat16


def swapped(x):
    return lax.ppermute(x, "core", [(0, 1), (1, 0)])


def passed_on(x):
    n = lax.axis_size(ROW)
    up = [(i, i + 2) for i in range(0, n - 2, 2)]
    down = [(i, i - 2) for i in range(3, n, 2)]
    return lax.ppermute(x, ROW, up + down)


def halo(features, weight):
    other = swapped(features)
    one = passed_on(jnp.stack([features, other]))
    two = passed_on(one)
    whole_weight = spread(weight, "col")
    last = swapped(two[1] + whole_weight[0, 0, 0] * 0)
    pieces = [(features, 0), (other, 1), (one, 2), (two, 4), (swapped(one), 6), (last, 8)]
    return pieces, whole_weight.reshape(-1, weight.shape[1])


def slots_of(tile_cols, tile_count, blocks_here):
    device = lax.axis_index(ROW)
    source = tile_cols // blocks_here
    chip = source // 2 - device // 2
    core = device % 2
    same = source % 2 == core
    second = jnp.where(same, 0, 1)
    own_side = (chip < 0) == (core == 0)
    one = jnp.where(own_side, 2 + second, 7 - second)
    two = jnp.where(own_side, 4 + second, 8)
    distance = jnp.abs(chip)
    group = jnp.where(distance == 0, second, jnp.where(distance == 1, one, two))
    slot = group * blocks_here + tile_cols % blocks_here
    keep = jnp.arange(tile_cols.shape[1], dtype=jnp.int32)[None, :] < tile_count[:, None]
    return jnp.where(keep, slot, 9 * blocks_here)


def tiles_kernel(starts, slots, *refs):
    pieces = refs[: len(starts)]
    vals_hbm, out, window, vals, piece_sems, vals_sems = refs[len(starts) :]
    blocks, count, tile, cols = vals.shape[0], vals.shape[1], vals.shape[2], window.shape[2]
    copies = [
        pltpu.make_async_copy(piece, window.at[pl.ds(start, piece.shape[0])], piece_sems.at[i])
        for i, (piece, start) in enumerate(zip(pieces, starts))
    ]
    for copy in copies:
        copy.start()
    span = blocks // vals_sems.shape[0]
    parts = [pl.ds(i * span, span) for i in range(vals_sems.shape[0])]
    fetches = [
        pltpu.make_async_copy(vals_hbm.at[part], vals.at[part], vals_sems.at[i])
        for i, part in enumerate(parts)
    ]
    for fetch in fetches:
        fetch.start()
    window[window.shape[0] - 1] = jnp.zeros((tile, cols), window.dtype)
    for copy in copies:
        copy.wait()
    for b in range(blocks):
        if b % span == 0:
            fetches[b // span].wait()
        total = jnp.zeros((tile, cols), F32)
        for t in range(0, count, 2):
            pair = jnp.concatenate([vals[b, t], vals[b, t + 1]], axis=1)
            rows = jnp.concatenate([window[slots[b, t]], window[slots[b, t + 1]]], axis=0)
            total += jnp.dot(pair, rows, preferred_element_type=F32)
        done = total.astype(out.dtype)
        for k in range(out.shape[0]):
            out[k, pl.ds(b * tile, tile), :] = done


def tiles(pieces, slots, tile_vals, times):
    blocks, count, tile, _ = tile_vals.shape
    cols = pieces[0][0].shape[-1]
    arrays = [x.reshape(-1, tile, cols) for x, _ in pieces]
    arrays[0] = pltpu.with_memory_space_constraint(arrays[0], pltpu.HBM)
    arrays[2] = pltpu.with_memory_space_constraint(arrays[2], pltpu.HBM)
    starts = [group * blocks for _, group in pieces]
    anywhere = pl.BlockSpec(memory_space=pl.ANY)
    hbm = pl.BlockSpec(memory_space=pltpu.HBM)
    return pl.pallas_call(
        functools.partial(tiles_kernel, starts),
        out_shape=jax.ShapeDtypeStruct((times, blocks * tile, cols), BF16),
        in_specs=[pl.BlockSpec(memory_space=pltpu.SMEM)] + [anywhere] * len(arrays) + [hbm],
        out_specs=pl.BlockSpec(memory_space=pltpu.VMEM),
        scratch_shapes=[
            pltpu.VMEM((9 * blocks + 1, tile, cols), BF16),
            pltpu.VMEM(tile_vals.shape, BF16),
            pltpu.SemaphoreType.DMA((len(arrays),)),
            pltpu.SemaphoreType.DMA((blocks // 2,)),
        ],
        compiler_params=pltpu.CompilerParams(vmem_limit_bytes=16 << 20),
        cost_estimate=pl.CostEstimate(
            flops=2 * blocks * count * tile * tile * cols, bytes_accessed=7 << 20, transcendentals=0
        ),
    )(slots, *arrays, pltpu.with_memory_space_constraint(tile_vals, pltpu.HBM))


def dense_kernel(me, agg, weight, cotangent, activated, grad, act, total):
    step = pl.program_id(0)
    mine = me[0]
    width = activated.shape[1]
    joined = jnp.concatenate([agg[k] for k in range(agg.shape[0])], axis=1)
    pre = jnp.dot(joined, weight[...], preferred_element_type=F32)
    sigma = 0.5 * jnp.tanh(0.5 * pre) + 0.5
    act[...] = pre * sigma
    activated[...] = act[:, pl.ds(pl.multiple_of(mine * width, width), width)].astype(BF16)
    dpre = (cotangent[...].astype(F32) * sigma * (1.0 + pre * (1.0 - sigma))).astype(BF16)
    part = lax.dot_general(agg[mine], dpre, (((0,), (0,)), ((), ())), preferred_element_type=F32)

    @pl.when(step == 0)
    def _():
        total[...] = part

    @pl.when(step > 0)
    def _():
        total[...] += part

    @pl.when(step == pl.num_programs(0) - 1)
    def _():
        grad[...] = total[...].astype(BF16)


def dense(agg, weight, cotangent):
    groups, rows, width = agg.shape
    f_out = weight.shape[1]
    block = 512
    me = lax.axis_index("col").astype(jnp.int32)[None]
    return pl.pallas_call(
        dense_kernel,
        out_shape=(
            jax.ShapeDtypeStruct((rows, f_out // groups), BF16),
            jax.ShapeDtypeStruct((width, f_out), BF16),
        ),
        grid=(rows // block,),
        in_specs=[
            pl.BlockSpec(memory_space=pltpu.SMEM),
            pl.BlockSpec((groups, block, width), lambda i: (0, i, 0)),
            pl.BlockSpec((groups * width, f_out), lambda i: (0, 0)),
            pl.BlockSpec((block, f_out), lambda i: (i, 0)),
        ],
        out_specs=(
            pl.BlockSpec((block, f_out // groups), lambda i: (i, 0)),
            pl.BlockSpec((width, f_out), lambda i: (0, 0)),
        ),
        scratch_shapes=[pltpu.VMEM((block, f_out), F32), pltpu.VMEM((width, f_out), F32)],
        compiler_params=pltpu.CompilerParams(vmem_limit_bytes=16 << 20),
    )(me, agg, weight, cotangent)


def spread(x, axes):
    n = lax.axis_size(axes)
    return exchanged(jnp.broadcast_to(x[None], (n,) + x.shape), axes)


def exchanged(x, axes):
    return lax.all_to_all(x, axes, 0, 0, tiled=True)


def summed_over_row(part):
    near = lax.axis_size(NEAR)
    rows, cols = part.shape
    pieces = exchanged(part.reshape(near, rows // near, cols), NEAR)
    piece = jnp.sum(pieces.astype(F32), 0).astype(BF16)
    whole = jnp.sum(spread(piece, FAR).astype(F32), 0).astype(BF16)
    return spread(whole, NEAR).reshape(rows, cols).astype(F32)


def shards(features, tile_vals, tile_cols, tile_count, weight, cotangent):
    groups = lax.axis_size("col")
    slots = slots_of(tile_cols, tile_count, tile_vals.shape[0])
    pieces, whole_weight = halo(features, weight)
    aggregated = tiles(pieces, slots, tile_vals, groups)
    activated, part = dense(exchanged(aggregated, "col"), whole_weight, cotangent)
    return activated, summed_over_row(part)


def solution(mesh):
    split = Mesh(mesh.devices.reshape(2, 8, 8, 2, 4), ROW + ("col",))
    return jax.shard_map(
        shards,
        mesh=split,
        in_specs=(
            P(ROW, "col"),
            P(ROW, None, None, None),
            P(ROW, None),
            P(ROW),
            P("col", None),
            P(ROW, None),
        ),
        out_specs=(P(ROW, "col"), P("col", None)),
        check_vma=False,
    )
```

```python
import functools

import jax
import jax.numpy as jnp
from jax import lax
from jax.experimental import pallas as pl
from jax.experimental.pallas import tpu as pltpu
from jax.sharding import Mesh, PartitionSpec as P

ROW = ("y_lo", "x", "z", "core")
NEAR = ("z", "core")
FAR = ("y_lo", "x")
F32 = jnp.float32
BF16 = jnp.bfloat16


def swapped(x):
    return lax.ppermute(x, "core", [(0, 1), (1, 0)])


def passed_on(x):
    n = lax.axis_size(ROW)
    up = [(i, i + 2) for i in range(0, n - 2, 2)]
    down = [(i, i - 2) for i in range(3, n, 2)]
    return lax.ppermute(x, ROW, up + down)


def halo(features, weight):
    other = swapped(features)
    one = passed_on(jnp.stack([features, other]))
    two = passed_on(one)
    whole_weight = spread(weight, "col")
    last = swapped(two[1] + whole_weight[0, 0, 0] * 0)
    pieces = [(features, 0), (other, 1), (one, 2), (two, 4), (swapped(one), 6), (last, 8)]
    return pieces, whole_weight.reshape(-1, weight.shape[1])


def slots_of(tile_cols, tile_count, blocks_here):
    device = lax.axis_index(ROW)
    source = tile_cols // blocks_here
    chip = source // 2 - device // 2
    core = device % 2
    same = source % 2 == core
    second = jnp.where(same, 0, 1)
    own_side = (chip < 0) == (core == 0)
    one = jnp.where(own_side, 2 + second, 7 - second)
    two = jnp.where(own_side, 4 + second, 8)
    distance = jnp.abs(chip)
    group = jnp.where(distance == 0, second, jnp.where(distance == 1, one, two))
    slot = group * blocks_here + tile_cols % blocks_here
    keep = jnp.arange(tile_cols.shape[1], dtype=jnp.int32)[None, :] < tile_count[:, None]
    return jnp.where(keep, slot, 9 * blocks_here)


def tiles_kernel(starts, slots, *refs):
    pieces = refs[: len(starts)]
    vals_hbm, out, window, vals, piece_sems, vals_sems = refs[len(starts) :]
    blocks, count, tile, cols = vals.shape[0], vals.shape[1], vals.shape[2], window.shape[2]
    copies = [
        pltpu.make_async_copy(piece, window.at[pl.ds(start, piece.shape[0])], piece_sems.at[i])
        for i, (piece, start) in enumerate(zip(pieces, starts))
    ]
    for copy in copies:
        copy.start()
    span = blocks // vals_sems.shape[0]
    parts = [pl.ds(i * span, span) for i in range(vals_sems.shape[0])]
    fetches = [
        pltpu.make_async_copy(vals_hbm.at[part], vals.at[part], vals_sems.at[i])
        for i, part in enumerate(parts)
    ]
    for fetch in fetches:
        fetch.start()
    window[window.shape[0] - 1] = jnp.zeros((tile, cols), window.dtype)
    for copy in copies:
        copy.wait()
    for b in range(blocks):
        if b % span == 0:
            fetches[b // span].wait()
        total = jnp.zeros((tile, cols), F32)
        for t in range(0, count, 2):
            pair = jnp.concatenate([vals[b, t], vals[b, t + 1]], axis=1)
            rows = jnp.concatenate([window[slots[b, t]], window[slots[b, t + 1]]], axis=0)
            total += jnp.dot(pair, rows, preferred_element_type=F32)
        out[pl.ds(b * tile, tile), :] = total.astype(out.dtype)


def tiles(pieces, slots, tile_vals):
    blocks, count, tile, _ = tile_vals.shape
    cols = pieces[0][0].shape[-1]
    arrays = [x.reshape(-1, tile, cols) for x, _ in pieces]
    arrays[0] = pltpu.with_memory_space_constraint(arrays[0], pltpu.HBM)
    arrays[2] = pltpu.with_memory_space_constraint(arrays[2], pltpu.HBM)
    starts = [group * blocks for _, group in pieces]
    anywhere = pl.BlockSpec(memory_space=pl.ANY)
    hbm = pl.BlockSpec(memory_space=pltpu.HBM)
    return pl.pallas_call(
        functools.partial(tiles_kernel, starts),
        out_shape=jax.ShapeDtypeStruct((blocks * tile, cols), BF16),
        in_specs=[pl.BlockSpec(memory_space=pltpu.SMEM)] + [anywhere] * len(arrays) + [hbm],
        out_specs=pl.BlockSpec(memory_space=pltpu.VMEM),
        scratch_shapes=[
            pltpu.VMEM((9 * blocks + 1, tile, cols), BF16),
            pltpu.VMEM(tile_vals.shape, BF16),
            pltpu.SemaphoreType.DMA((len(arrays),)),
            pltpu.SemaphoreType.DMA((blocks // 2,)),
        ],
        compiler_params=pltpu.CompilerParams(vmem_limit_bytes=16 << 20),
        cost_estimate=pl.CostEstimate(
            flops=2 * blocks * count * tile * tile * cols, bytes_accessed=7 << 20, transcendentals=0
        ),
    )(slots, *arrays, pltpu.with_memory_space_constraint(tile_vals, pltpu.HBM))


def dense_kernel(me, weight, cotangent, *refs):
    groups = weight.shape[0] // refs[0].shape[1]
    aggs = refs[:groups]
    activated, grad, turned, act, total = refs[groups:]
    step = pl.program_id(0)
    mine = me[0]
    width = activated.shape[1]

    @pl.when(step == 0)
    def _():
        for by in range(groups):
            start = pl.multiple_of(lax.rem(mine + by, groups) * width, width)
            turned[pl.ds(by * width, width), :] = weight[pl.ds(start, width), :]

    joined = jnp.concatenate([agg[...] for agg in aggs], axis=1)
    pre = jnp.dot(joined, turned[...], preferred_element_type=F32)
    sigma = 0.5 * jnp.tanh(0.5 * pre) + 0.5
    act[...] = pre * sigma
    activated[...] = act[:, pl.ds(pl.multiple_of(mine * width, width), width)].astype(BF16)
    dpre = (cotangent[...].astype(F32) * sigma * (1.0 + pre * (1.0 - sigma))).astype(BF16)
    part = lax.dot_general(aggs[0][...], dpre, (((0,), (0,)), ((), ())), preferred_element_type=F32)

    @pl.when(step == 0)
    def _():
        total[...] = part

    @pl.when(step > 0)
    def _():
        total[...] += part

    @pl.when(step == pl.num_programs(0) - 1)
    def _():
        grad[...] = total[...].astype(BF16)


def dense(aggs, weight, cotangent):
    groups, (rows, width) = len(aggs), aggs[0].shape
    f_out = weight.shape[1]
    block = 512
    me = lax.axis_index("col").astype(jnp.int32)[None]
    return pl.pallas_call(
        dense_kernel,
        out_shape=(
            jax.ShapeDtypeStruct((rows, f_out // groups), BF16),
            jax.ShapeDtypeStruct((width, f_out), BF16),
        ),
        grid=(rows // block,),
        in_specs=[
            pl.BlockSpec(memory_space=pltpu.SMEM),
            pl.BlockSpec((groups * width, f_out), lambda i: (0, 0)),
            pl.BlockSpec((block, f_out), lambda i: (i, 0)),
        ]
        + [pl.BlockSpec((block, width), lambda i: (i, 0))] * groups,
        out_specs=(
            pl.BlockSpec((block, f_out // groups), lambda i: (i, 0)),
            pl.BlockSpec((width, f_out), lambda i: (0, 0)),
        ),
        scratch_shapes=[
            pltpu.VMEM((groups * width, f_out), BF16),
            pltpu.VMEM((block, f_out), F32),
            pltpu.VMEM((width, f_out), F32),
        ],
        compiler_params=pltpu.CompilerParams(vmem_limit_bytes=16 << 20),
    )(me, weight, cotangent, *aggs)


def turned(x, axis):
    n = lax.axis_size(axis)
    return [x] + [lax.ppermute(x, axis, [((i + by) % n, i) for i in range(n)]) for by in range(1, n)]


def spread(x, axes):
    n = lax.axis_size(axes)
    return exchanged(jnp.broadcast_to(x[None], (n,) + x.shape), axes)


def exchanged(x, axes):
    return lax.all_to_all(x, axes, 0, 0, tiled=True)


def summed_over_row(part):
    near = lax.axis_size(NEAR)
    rows, cols = part.shape
    pieces = exchanged(part.reshape(near, rows // near, cols), NEAR)
    piece = jnp.sum(pieces.astype(F32), 0).astype(BF16)
    whole = jnp.sum(spread(piece, FAR).astype(F32), 0).astype(BF16)
    return spread(whole, NEAR).reshape(rows, cols).astype(F32)


def shards(features, tile_vals, tile_cols, tile_count, weight, cotangent):
    slots = slots_of(tile_cols, tile_count, tile_vals.shape[0])
    pieces, whole_weight = halo(features, weight)
    aggregated = tiles(pieces, slots, tile_vals)
    activated, part = dense(turned(aggregated, "col"), whole_weight, cotangent)
    return activated, summed_over_row(part)


def solution(mesh):
    split = Mesh(mesh.devices.reshape(2, 8, 8, 2, 4), ROW + ("col",))
    return jax.shard_map(
        shards,
        mesh=split,
        in_specs=(
            P(ROW, "col"),
            P(ROW, None, None, None),
            P(ROW, None),
            P(ROW),
            P("col", None),
            P(ROW, None),
        ),
        out_specs=(P(ROW, "col"), P("col", None)),
        check_vma=False,
    )
```

```python
import functools

import jax
import jax.numpy as jnp
from jax import lax
from jax.experimental import pallas as pl
from jax.experimental.pallas import tpu as pltpu
from jax.sharding import Mesh, PartitionSpec as P

ROW = ("y_lo", "x", "z", "core")
NEAR = ("z", "core")
FAR = ("y_lo", "x")
F32 = jnp.float32
BF16 = jnp.bfloat16


def swapped(x):
    return lax.ppermute(x, "core", [(0, 1), (1, 0)])


def passed_on(x):
    n = lax.axis_size(ROW)
    up = [(i, i + 2) for i in range(0, n - 2, 2)]
    down = [(i, i - 2) for i in range(3, n, 2)]
    return lax.ppermute(x, ROW, up + down)


def halo(features):
    one = passed_on(features)
    other = swapped(features)
    one_other = passed_on(other)
    two = passed_on(one)
    two_other = passed_on(one_other)
    across = swapped(jnp.stack([one, one_other]))
    last = swapped(two_other)
    arrays = [features, other, one, one_other, two, two_other, across, last]
    return list(zip(arrays, [0, 1, 2, 3, 4, 5, 6, 8]))


def slots_of(tile_cols, tile_count, blocks_here):
    device = lax.axis_index(ROW)
    source = tile_cols // blocks_here
    chip = source // 2 - device // 2
    core = device % 2
    same = source % 2 == core
    second = jnp.where(same, 0, 1)
    own_side = (chip < 0) == (core == 0)
    one = jnp.where(own_side, 2 + second, 7 - second)
    two = jnp.where(own_side, 4 + second, 8)
    distance = jnp.abs(chip)
    group = jnp.where(distance == 0, second, jnp.where(distance == 1, one, two))
    slot = group * blocks_here + tile_cols % blocks_here
    keep = jnp.arange(tile_cols.shape[1], dtype=jnp.int32)[None, :] < tile_count[:, None]
    return jnp.where(keep, slot, 9 * blocks_here)


def tiles_kernel(starts, slots, *refs):
    pieces = refs[: len(starts)]
    vals_hbm, _, out, window, vals, piece_sems, vals_sems = refs[len(starts) :]
    blocks, count, tile, cols = vals.shape[0], vals.shape[1], vals.shape[2], window.shape[2]
    copies = [
        pltpu.make_async_copy(piece, window.at[pl.ds(start, piece.shape[0])], piece_sems.at[i])
        for i, (piece, start) in enumerate(zip(pieces, starts))
    ]
    for copy in copies:
        copy.start()
    span = blocks // vals_sems.shape[0]
    parts = [pl.ds(i * span, span) for i in range(vals_sems.shape[0])]
    fetches = [
        pltpu.make_async_copy(vals_hbm.at[part], vals.at[part], vals_sems.at[i])
        for i, part in enumerate(parts)
    ]
    for fetch in fetches:
        fetch.start()
    window[window.shape[0] - 1] = jnp.zeros((tile, cols), window.dtype)
    for copy in copies:
        copy.wait()
    for b in range(blocks):
        if b % span == 0:
            fetches[b // span].wait()
        total = jnp.zeros((tile, cols), F32)
        for t in range(0, count, 2):
            pair = jnp.concatenate([vals[b, t], vals[b, t + 1]], axis=1)
            rows = jnp.concatenate([window[slots[b, t]], window[slots[b, t + 1]]], axis=0)
            total += jnp.dot(pair, rows, preferred_element_type=F32)
        done = total.astype(out.dtype)
        for k in range(out.shape[0]):
            out[k, pl.ds(b * tile, tile), :] = done


def tiles(pieces, slots, tile_vals, weight):
    times = weight.shape[0]
    blocks, count, tile, _ = tile_vals.shape
    cols = pieces[0][0].shape[-1]
    arrays = [x.reshape(-1, tile, cols) for x, _ in pieces]
    arrays[0] = pltpu.with_memory_space_constraint(arrays[0], pltpu.HBM)
    arrays[7] = pltpu.with_memory_space_constraint(arrays[7], pltpu.HBM)
    starts = [group * blocks for _, group in pieces]
    anywhere = pl.BlockSpec(memory_space=pl.ANY)
    hbm = pl.BlockSpec(memory_space=pltpu.HBM)
    return pl.pallas_call(
        functools.partial(tiles_kernel, starts),
        out_shape=jax.ShapeDtypeStruct((times, blocks * tile, cols), BF16),
        in_specs=[pl.BlockSpec(memory_space=pltpu.SMEM)] + [anywhere] * len(arrays) + [hbm, anywhere],
        out_specs=pl.BlockSpec(memory_space=pltpu.VMEM),
        scratch_shapes=[
            pltpu.VMEM((9 * blocks + 1, tile, cols), BF16),
            pltpu.VMEM(tile_vals.shape, BF16),
            pltpu.SemaphoreType.DMA((len(arrays),)),
            pltpu.SemaphoreType.DMA((blocks // 2,)),
        ],
        compiler_params=pltpu.CompilerParams(vmem_limit_bytes=16 << 20),
        cost_estimate=pl.CostEstimate(
            flops=2 * blocks * count * tile * tile * cols, bytes_accessed=7 << 20, transcendentals=0
        ),
    )(slots, *arrays, pltpu.with_memory_space_constraint(tile_vals, pltpu.HBM), weight)


def dense_kernel(me, agg, weight, cotangent, activated, grad, act, total):
    step = pl.program_id(0)
    mine = me[0]
    width = activated.shape[1]
    joined = jnp.concatenate([agg[k] for k in range(agg.shape[0])], axis=1)
    pre = jnp.dot(joined, weight[...], preferred_element_type=F32)
    sigma = 0.5 * jnp.tanh(0.5 * pre) + 0.5
    act[...] = pre * sigma
    activated[...] = act[:, pl.ds(pl.multiple_of(mine * width, width), width)].astype(BF16)
    dpre = (cotangent[...].astype(F32) * sigma * (1.0 + pre * (1.0 - sigma))).astype(BF16)
    part = lax.dot_general(agg[mine], dpre, (((0,), (0,)), ((), ())), preferred_element_type=F32)

    @pl.when(step == 0)
    def _():
        total[...] = part

    @pl.when(step > 0)
    def _():
        total[...] += part

    @pl.when(step == pl.num_programs(0) - 1)
    def _():
        grad[...] = total[...].astype(BF16)


def dense(agg, weight, cotangent):
    groups, rows, width = agg.shape
    f_out = weight.shape[1]
    block = 512
    me = lax.axis_index("col").astype(jnp.int32)[None]
    return pl.pallas_call(
        dense_kernel,
        out_shape=(
            jax.ShapeDtypeStruct((rows, f_out // groups), BF16),
            jax.ShapeDtypeStruct((width, f_out), BF16),
        ),
        grid=(rows // block,),
        in_specs=[
            pl.BlockSpec(memory_space=pltpu.SMEM),
            pl.BlockSpec((groups, block, width), lambda i: (0, i, 0)),
            pl.BlockSpec((groups * width, f_out), lambda i: (0, 0)),
            pl.BlockSpec((block, f_out), lambda i: (i, 0)),
        ],
        out_specs=(
            pl.BlockSpec((block, f_out // groups), lambda i: (i, 0)),
            pl.BlockSpec((width, f_out), lambda i: (0, 0)),
        ),
        scratch_shapes=[pltpu.VMEM((block, f_out), F32), pltpu.VMEM((width, f_out), F32)],
        compiler_params=pltpu.CompilerParams(vmem_limit_bytes=16 << 20),
    )(me, agg, weight, cotangent)


def spread(x, axes):
    n = lax.axis_size(axes)
    return exchanged(jnp.broadcast_to(x[None], (n,) + x.shape), axes)


def exchanged(x, axes):
    return lax.all_to_all(x, axes, 0, 0, tiled=True)


def summed_over_row(part):
    near = lax.axis_size(NEAR)
    rows, cols = part.shape
    pieces = exchanged(part.reshape(near, rows // near, cols), NEAR)
    piece = jnp.sum(pieces.astype(F32), 0).astype(BF16)
    whole = jnp.sum(spread(piece, FAR).astype(F32), 0).astype(BF16)
    return spread(whole, NEAR).reshape(rows, cols).astype(F32)


def shards(features, tile_vals, tile_cols, tile_count, weight, cotangent):
    slots = slots_of(tile_cols, tile_count, tile_vals.shape[0])
    whole_weight = spread(weight, "col")
    aggregated = tiles(halo(features), slots, tile_vals, whole_weight)
    whole_weight = whole_weight.reshape(-1, weight.shape[1])
    activated, part = dense(exchanged(aggregated, "col"), whole_weight, cotangent)
    return activated, summed_over_row(part)


def solution(mesh):
    split = Mesh(mesh.devices.reshape(2, 8, 8, 2, 4), ROW + ("col",))
    return jax.shard_map(
        shards,
        mesh=split,
        in_specs=(
            P(ROW, "col"),
            P(ROW, None, None, None),
            P(ROW, None),
            P(ROW),
            P("col", None),
            P(ROW, None),
        ),
        out_specs=(P(ROW, "col"), P("col", None)),
        check_vma=False,
    )
```
